32 devices in a mesh: groups: 2 (over y), ctx: 4 (over z), peer: 4 (over x, core).
Axes of the slice: x: 2, y: 2, z: 4, core: 2. Of those that a mesh axis runs over, the one named last changes fastest.
Arguments:
- queries: bfloat16 [4, 4, 64, 128], P('groups'), parts along dimension 0, may hold values from -170 to 170
- key_cache: bfloat16 [4, 256, 8, 64, 128], P('groups', ('ctx', 'peer')), parts along dimension 0, may hold values from -6 to 6
- value_cache: bfloat16 [4, 256, 8, 64, 128], P('groups', ('ctx', 'peer')), parts along dimension 0, may hold values from -6 to 6
- page_list: int32 [4, 4, 8, 64], P('groups'), parts along dimension 0, may hold values from 0 to 255, as said below
- out_weight: bfloat16 [8192, 8192], P('ctx'), may hold values from -0.09375 to 0.09375
Outputs:
- layer_out: float32 [4, 4, 8192], P('groups', 'peer', 'ctx'), parts along dimension 0
The draws below stay inside these ranges and needn't reach their ends.
There are 2 independent parts, one for each index of `groups`. The reference program is written for one: setup_inputs(seed, part) draws one part's arguments, and reference() takes and returns one part's arrays. A program takes and returns all parts, laid end to end along the dimension named above; an argument that names none is the same for every part. Nothing has to cross between parts.
Inputs may be any that keep to these rules, and one draw needn't show every extreme that they name: `page_list`: for each sequence, step and key head the 64 ids are distinct; each block of 16 consecutive pages holds at most 8 of them, and some block holds exactly 8.
All inputs are finite; a program needn't handle non-finite values.
Results may differ from the reference program's by a relative error of at most 0.005.
Values sent between devices are 32-bit elements; how exact they have to be, the bound alone decides.
A program may use at most 128 MiB of HBM per device.

```python
import math
import jax
import jax.numpy as jnp
from jax import lax

HQ = 64
KVH = 8
HD = 128
D = 8192
PAGE = 64
STEPS = 4
SEQS = 2
PAGES_DEV = 16
MOST = 8
PAGES = 256
NSEL = 64


def draw_queries(key, part):
    key = jax.random.fold_in(key, 3)
    scale_key, value_key = jax.random.split(key, 2)
    full_shape = (SEQS, STEPS, HQ, HD)
    spread = jnp.exp(jax.random.uniform(scale_key, (SEQS, STEPS, HQ, 1), minval=math.log(0.5), maxval=math.log(4.0)))
    raw_values = jax.random.truncated_normal(value_key, -5.0, 5.0, full_shape)
    return (raw_values * spread).astype(jnp.bfloat16)


def draw_page_list(key, part):
    key = jax.random.fold_in(key, 7)
    partition_count = PAGES // PAGES_DEV

    def one_row(row_random_key):
        shuffle_random_key, extra_random_key, popular_random_key, ordering_random_key = jax.random.split(row_random_key, 4)
        orders = jax.vmap(lambda sub_key: jax.random.permutation(sub_key, PAGES_DEV))(jax.random.split(shuffle_random_key, partition_count))
        eligible = orders < MOST
        score_boosts = jax.random.randint(extra_random_key, (partition_count,), 0, 3)
        hottest = jax.random.randint(popular_random_key, (), 0, partition_count)
        score_boosts = jnp.where(jnp.arange(partition_count) == hottest, 3, score_boosts)
        jitter = jax.random.randint(ordering_random_key, (partition_count, PAGES_DEV), 0, 2 ** 15)
        page_index = jnp.arange(PAGES, dtype=jnp.int32).reshape(partition_count, PAGES_DEV)
        scores_int = jnp.where(eligible, (score_boosts[:, None] * 2 ** 15 + jitter) * PAGES + page_index, -1 - page_index)
        picked = lax.top_k(scores_int.reshape(-1), NSEL)[1]
        return picked.astype(jnp.int32)
    row_keys = jax.random.split(key, SEQS * STEPS * KVH)
    return jax.vmap(one_row)(row_keys).reshape(SEQS, STEPS, KVH, NSEL)


def strengthened(values, own_key, source, target, blocks, factor):
    def block_of(dim):
        return (jnp.arange(values.shape[dim]) // (values.shape[dim] // blocks)).reshape((-1,) + (1,) * (values.ndim - 1 - dim))

    first = jax.random.permutation(own_key, blocks)[block_of(target)]
    other_side = (block_of(target) + blocks // 2) % blocks
    return jnp.where((block_of(source) == first) | (block_of(source) == other_side), factor * values, values)


def block_levels(key, shape, pieces, least, largest):
    def one(dim, parts):
        heights = jax.random.uniform(jax.random.fold_in(jax.random.fold_in(key, 6), dim), (parts,), jnp.float32, least / len(pieces), largest / len(pieces))
        return jnp.repeat(jnp.exp(heights), shape[dim] // parts).reshape((-1,) + (1,) * (len(shape) - dim - 1))

    loudness = one(*pieces[0])
    for cut in pieces[1:]:
        loudness = loudness * one(*cut)
    return loudness


def bell_draw(key, dims, scale, most, cuts=(), held_as=jnp.bfloat16):
    result = scale * jax.random.normal(key, dims, jnp.float32)
    if cuts:
        result = result * block_levels(key, dims, cuts, -0.22, 0.18)
    return jnp.clip(result, -most, most).astype(held_as)


def bell_draw_with(own_key, extent, width, most, cuts, heavy, kind=jnp.bfloat16):
    entries = width * jax.random.normal(own_key, extent, jnp.float32)
    if cuts:
        entries = entries * block_levels(own_key, extent, cuts, -0.22, 0.18)
    return jnp.clip(strengthened(entries, jax.random.fold_in(own_key, 3), *heavy), -most, most).astype(kind)


def setup_inputs(seed: int = 0, part: int = 0) -> dict:
    splits = jax.random.split(jax.random.key(seed), 6)
    part_keys = jax.random.split(jax.random.fold_in(splits[5], part), 6)
    queries = draw_queries(jax.random.fold_in(jax.random.fold_in(splits[5], part), 71), part)
    key_cache = bell_draw(part_keys[1], (SEQS, PAGES, KVH, PAGE, HD), 1.0, 6.0, ((1, 16),))
    value_cache = bell_draw(part_keys[2], (SEQS, PAGES, KVH, PAGE, HD), 1.0, 6.0, ((1, 16),))
    page_list = draw_page_list(jax.random.fold_in(jax.random.fold_in(splits[5], part), 71), part)
    out_weight = bell_draw_with(splits[4], (HQ * HD, D), (HQ * HD) ** -0.5, 0.09375, ((0, 4),), (0, 1, 4, 2.0))
    return {"queries": queries, "key_cache": key_cache, "value_cache": value_cache, "page_list": page_list, "out_weight": out_weight}


def reference(queries, key_cache, value_cache, page_list, out_weight):
    group_size = HQ // KVH
    inv_root = HD ** -0.5

    def attend_one(flat_index):
        seq_id = flat_index // (STEPS * KVH)
        step_id = (flat_index // KVH) % STEPS
        head_id = flat_index % KVH
        page_ids = page_list[seq_id, step_id, head_id]
        page_keys = key_cache[seq_id, page_ids, head_id].reshape(NSEL * PAGE, HD)
        page_values = value_cache[seq_id, page_ids, head_id].reshape(NSEL * PAGE, HD)
        query_rows = lax.dynamic_slice(queries, (seq_id, step_id, head_id * group_size, jnp.int32(0)), (1, 1, group_size, HD)).reshape(group_size, HD)
        scores = lax.dot_general(query_rows, page_keys, (((1,), (1,)), ((), ())), preferred_element_type=jnp.float32) * inv_root
        highest = jnp.max(scores, axis=1, keepdims=True)
        weights = jnp.exp(scores - highest)
        totals = jnp.sum(weights, axis=1, keepdims=True)
        blended = jnp.dot(weights.astype(jnp.bfloat16), page_values, preferred_element_type=jnp.float32) / totals
        return blended.astype(jnp.bfloat16)

    attended = lax.map(attend_one, jnp.arange(SEQS * STEPS * KVH, dtype=jnp.int32))
    attended = attended.reshape(SEQS * STEPS, HQ * HD)
    layer_out = jnp.dot(attended, out_weight, preferred_element_type=jnp.float32)
    return layer_out.reshape(SEQS, STEPS, D)
```

```python
import functools
import math

import jax
import jax.numpy as jnp
from jax import lax
from jax.experimental import pallas as pl
from jax.experimental.pallas import tpu as pltpu
from jax.sharding import PartitionSpec as P

masked_score = -1e30
least_maximum = -1e20
LANES = 128
HALF = LANES // 2


def kernel(
    dims,
    q_ref, list_ref, key_ref, value_ref, weight_ref, out_ref,
    kbuf, vbuf, wbuf, qs, mask, send_a, recv_a, send_b, recv_b, gat, send_c, recv_c,
    k_sem, v_sem, w_sem, sa_sem, ra_sem, sb_sem, rb_sem, sg_sem, rg_sem, sc_sem, rc_sem,
):
    C, N, B, S, KV, G, HD, PG, PAGE, D = dims
    SS = S // N
    KC = max(1, KV // C)
    NB = KV // KC
    R = C // NB
    HS = KV * G // C
    Q = C // N
    U = SS * B * KC
    rows = U * G
    tokens = PG * PAGE
    scale = HD ** (-0.5) * math.log2(math.e)
    c = lax.axis_index("ctx")
    p = lax.axis_index("peer")
    own = c // R
    place = lax.rem(c, R)

    def block_of(i):
        return lax.rem(own + 1 + i, NB)

    loads = []
    for i in range(NB):
        heads = pl.ds(block_of(i) * KC, KC)
        loads.append((
            pltpu.make_async_copy(key_ref.at[:, :, heads], kbuf.at[i], k_sem.at[i]),
            pltpu.make_async_copy(value_ref.at[:, :, heads], vbuf.at[i], v_sem.at[i]),
        ))
    for pair in loads:
        pair[0].start()
        pair[1].start()
    columns = pl.ds(pl.multiple_of(p * (D // N), LANES), D // N)
    w_load = pltpu.make_async_copy(weight_ref.at[:, columns], wbuf, w_sem)
    w_load.start()

    barrier = pltpu.get_barrier_semaphore()
    for dc in range(C):
        for dp in range(N):
            if dc or dp:
                pl.semaphore_signal(
                    barrier, inc=1,
                    device_id={"ctx": lax.rem(c + dc, C), "peer": lax.rem(p + dp, N)},
                    device_id_type=pl.DeviceIdType.MESH,
                )

    for b in range(B):
        for s in range(S):
            some = q_ref[b, s].astype(jnp.float32)
            for h in range(KV):
                qs[h, b, s * G:(s + 1) * G, :] = some[h * G:(h + 1) * G]
    first = (c * N + p) * PG
    ids = list_ref[...].reshape(B * S * KV, list_ref.shape[3])
    per_tile = LANES // PAGE
    lane_page = lax.broadcasted_iota(jnp.int32, (ids.shape[1], LANES), 1) // PAGE
    for j in range(tokens // LANES):
        listed = jnp.zeros((B * S * KV, LANES), jnp.float32)
        for k in range(per_tile):
            equal = jnp.where(ids == first + (j * per_tile + k), 1.0, 0.0).astype(jnp.bfloat16)
            spread = jnp.where(lane_page == k, 1.0, 0.0).astype(jnp.bfloat16)
            listed += jnp.dot(equal, spread, preferred_element_type=jnp.float32)
        mask[:, j * LANES:(j + 1) * LANES] = listed

    lane = lax.broadcasted_iota(jnp.int32, (G, LANES), 1)

    def attend(i):
        blk = block_of(i)
        tiles = [jnp.zeros((G, LANES), jnp.float32)] * N
        loads[i][0].wait()
        loads[i][1].wait()
        for b in range(B):
            for kc in range(KC):
                h = blk * KC + kc
                q = qs[h, b].astype(jnp.bfloat16)
                keys = kbuf[i, b, :, kc].reshape(tokens, HD)
                values = vbuf[i, b, :, kc].reshape(tokens, HD)
                score = lax.dot_general(
                    q, keys, (((1,), (1,)), ((), ())), preferred_element_type=jnp.float32
                )
                listed = jnp.concatenate([
                    jnp.broadcast_to(mask[pl.ds((b * S + s) * KV + h, 1), :], (G, tokens))
                    for s in range(S)
                ], axis=0)
                score = jnp.where(listed > 0.5, score * scale, masked_score)
                top = jnp.maximum(jnp.max(score, axis=1, keepdims=True), least_maximum)
                weights = jnp.exp2(score - top)
                total = jnp.sum(weights, axis=1, keepdims=True)
                blended = jnp.dot(
                    weights.astype(jnp.bfloat16), values, preferred_element_type=jnp.float32
                )
                for s in range(S):
                    n, ss = divmod(s, SS)
                    u = (ss * B + b) * KC + kc
                    part = slice(s * G, (s + 1) * G)
                    send_a[i, n, u * G:(u + 1) * G, :] = blended[part]
                    tiles[n] = jnp.where(
                        lane == u, top[part], jnp.where(lane == HALF + u, total[part], tiles[n])
                    )
        for n in range(N):
            send_a[i, n, rows:rows + G, :] = tiles[n]

    def copies_a(i):
        made = []
        for d in range(1, N):
            to = lax.rem(p + d, N)
            made.append(pltpu.make_async_remote_copy(
                src_ref=send_a.at[i, to], dst_ref=recv_a.at[i, d - 1],
                send_sem=sa_sem.at[i, d - 1], recv_sem=ra_sem.at[i, d - 1],
                device_id={"peer": to}, device_id_type=pl.DeviceIdType.MESH,
            ))
        return made

    def copies_b(i):
        made = []
        for dr in range(R):
            if i == NB - 1 and dr == 0:
                continue
            slot = i * R + dr - (1 if i == NB - 1 else 0)
            to = block_of(i) * R + lax.rem(place + dr, R)
            made.append(pltpu.make_async_remote_copy(
                src_ref=send_b.at[i], dst_ref=recv_b.at[slot],
                send_sem=sb_sem.at[slot], recv_sem=rb_sem.at[slot],
                device_id={"ctx": to}, device_id_type=pl.DeviceIdType.MESH,
            ))
        return made

    def factors(tiles):
        top = functools.reduce(jnp.maximum, tiles)
        scales = [jnp.exp2(t - top) for t in tiles]
        total = sum(f * pltpu.roll(t, HALF, 1) for f, t in zip(scales, tiles))
        return top, scales, total

    def blend(parts, scales, u):
        return sum(
            part[u * G:(u + 1) * G, :] * f[:, u:u + 1] for part, f in zip(parts, scales)
        )

    def fold_a(i):
        parts = [send_a.at[i, p]] + [recv_a.at[i, d] for d in range(N - 1)]
        tiles = [part[rows:rows + G, :] for part in parts]
        top, scales, total = factors(tiles)
        for u in range(U):
            send_b[i, u * G:(u + 1) * G, :] = blend(parts, scales, u)
        send_b[i, rows:rows + G, :] = jnp.where(lane < HALF, top, pltpu.roll(total, HALF, 1))

    all_a, all_b = [], []
    for i in range(NB + 1):
        if i < NB:
            attend(i)
            if i == 0:
                pl.semaphore_wait(barrier, C * N - 1)
            all_a.append(copies_a(i))
            for copy in all_a[i]:
                copy.start()
        if i > 0:
            for copy in all_a[i - 1]:
                copy.wait_recv()
            fold_a(i - 1)
            made = copies_b(i - 1)
            for copy in made:
                copy.start()
            all_b += made

    for copy in all_b:
        copy.wait_recv()
    parts = [send_b.at[NB - 1]] + [recv_b.at[d] for d in range(C - 1)]
    top, scales, total = factors([part[rows:rows + G, :] for part in parts])
    scales = [f / total for f in scales]
    mine = pl.ds(pl.multiple_of(p * rows, 8), rows)
    attended = jnp.concatenate([blend(parts, scales, u) for u in range(U)], axis=0)
    gat[mine, :] = attended
    all_g = []
    for d in range(1, N):
        to = lax.rem(p + d, N)
        all_g.append(pltpu.make_async_remote_copy(
            src_ref=gat.at[mine], dst_ref=gat.at[mine],
            send_sem=sg_sem.at[d - 1], recv_sem=rg_sem.at[d - 1],
            device_id={"peer": to}, device_id_type=pl.DeviceIdType.MESH,
        ))
    for copy in all_g:
        copy.start()
    w_load.wait()
    for d in range(1, N):
        theirs = gat.at[pl.ds(pl.multiple_of(lax.rem(p + N - d, N) * rows, 8), rows)]
        pltpu.make_async_remote_copy(
            src_ref=theirs, dst_ref=theirs,
            send_sem=sg_sem.at[d - 1], recv_sem=rg_sem.at[d - 1],
            device_id={"peer": lax.rem(p + d, N)}, device_id_type=pl.DeviceIdType.MESH,
        ).wait_recv()

    left = jnp.concatenate([
        gat[pl.ds((place * HS if R > 1 else 0) + j, S * B, stride=KC * G), :] for j in range(HS)
    ], axis=1).astype(jnp.bfloat16)
    product = jnp.dot(left, wbuf[...], preferred_element_type=jnp.float32)
    width = D // C
    for q in range(Q):
        for n in range(N):
            send_c[q, n] = product[n * SS * B:(n + 1) * SS * B, q * width:(q + 1) * width]

    def copy_c(q, dn):
        to = lax.rem(p + dn, N)
        return pltpu.make_async_remote_copy(
            src_ref=send_c.at[q, to], dst_ref=recv_c.at[c],
            send_sem=sc_sem.at[q, dn], recv_sem=rc_sem.at[c],
            device_id={"ctx": p * Q + q, "peer": to}, device_id_type=pl.DeviceIdType.MESH,
        )

    for q in range(Q):
        for dn in range(1, N):
            copy_c(q, dn).start()

        @pl.when(p * Q + q != c)
        def _():
            copy_c(q, 0).start()

        @pl.when(p * Q + q == c)
        def _():
            recv_c[c] = send_c[q, p]

    def wait_c(source):
        pltpu.make_async_remote_copy(
            src_ref=send_c.at[0, 0], dst_ref=recv_c.at[source],
            send_sem=sc_sem.at[0, 0], recv_sem=rc_sem.at[source],
            device_id={"ctx": source, "peer": c // Q}, device_id_type=pl.DeviceIdType.MESH,
        ).wait_recv()

    for dc in range(1, C):
        wait_c(lax.rem(c + dc, C))

    @pl.when(p != c // Q)
    def _():
        wait_c(c)

    out_ref[...] = functools.reduce(jnp.add, [recv_c[k] for k in range(C)])

    for copies in all_a:
        for copy in copies:
            copy.wait_send()
    for copy in all_b + all_g:
        copy.wait_send()
    for q in range(Q):
        for dn in range(1, N):
            copy_c(q, dn).wait_send()

        @pl.when(p * Q + q != c)
        def _():
            copy_c(q, 0).wait_send()


def body(queries, key_cache, value_cache, page_list, out_weight):
    B, S, HQ, HD = queries.shape
    PG, KV, PAGE = key_cache.shape[1:4]
    D = out_weight.shape[1]
    C = lax.axis_size("ctx")
    N = lax.axis_size("peer")
    G = HQ // KV
    SS = S // N
    KC = max(1, KV // C)
    NB = KV // KC
    Q = C // N
    rows = SS * B * KC * G
    f32, bf16 = jnp.float32, jnp.bfloat16
    dma = pltpu.SemaphoreType.DMA
    dims = (C, N, B, S, KV, G, HD, PG, PAGE, D)
    vmem = pl.BlockSpec(memory_space=pltpu.VMEM)
    hbm = pl.BlockSpec(memory_space=pl.ANY)
    out = pl.pallas_call(
        functools.partial(kernel, dims),
        out_shape=jax.ShapeDtypeStruct((SS * B, D // C), f32),
        in_specs=[vmem, vmem, hbm, hbm, hbm],
        out_specs=vmem,
        scratch_shapes=[
            pltpu.VMEM((NB, B, PG, KC, PAGE, HD), bf16),
            pltpu.VMEM((NB, B, PG, KC, PAGE, HD), bf16),
            pltpu.VMEM((out_weight.shape[0], D // N), bf16),
            pltpu.VMEM((KV, B, S * G, HD), f32),
            pltpu.VMEM((B * S * KV, PG * PAGE), f32),
            pltpu.VMEM((NB, N, rows + G, HD), f32),
            pltpu.VMEM((NB, N - 1, rows + G, HD), f32),
            pltpu.VMEM((NB, rows + G, HD), f32),
            pltpu.VMEM((C - 1, rows + G, HD), f32),
            pltpu.VMEM((N * rows, HD), f32),
            pltpu.VMEM((Q, N, SS * B, D // C), f32),
            pltpu.VMEM((C, SS * B, D // C), f32),
            dma((NB,)), dma((NB,)), dma,
            dma((NB, N - 1)), dma((NB, N - 1)),
            dma((C - 1,)), dma((C - 1,)),
            dma((N - 1,)), dma((N - 1,)),
            dma((Q, N)), dma((C,)),
        ],
        compiler_params=pltpu.CompilerParams(
            collective_id=0, has_side_effects=True, vmem_limit_bytes=48 * 2**20
        ),
        name="paged_attention_projection",
    )(queries, page_list, key_cache, value_cache, out_weight)
    return out.reshape(SS, B, D // C).swapaxes(0, 1)


def solution(mesh):
    in_specs = (
        P("groups", None, None, None),
        P("groups", ("ctx", "peer"), None, None, None),
        P("groups", ("ctx", "peer"), None, None, None),
        P("groups", None, None, None),
        P("ctx", None),
    )
    out_specs = P("groups", "peer", "ctx")
    return jax.shard_map(body, mesh=mesh, in_specs=in_specs, out_specs=out_specs, check_vma=False)
```

```python
import functools
import math

import jax
import jax.numpy as jnp
from jax import lax
from jax.experimental import pallas as pl
from jax.experimental.pallas import tpu as pltpu
from jax.sharding import PartitionSpec as P

masked_score = -1e30
least_maximum = -1e20
LANES = 128
HALF = LANES // 2


def kernel(
    dims,
    q_ref, list_ref, key_ref, value_ref, weight_ref, out_ref,
    kbuf, vbuf, wbuf, qs, mask, send_a, recv_a, send_b, recv_b, gat, send_c, recv_c,
    k_sem, v_sem, w_sem, sa_sem, ra_sem, sb_sem, rb_sem, sg_sem, rg_sem, sc_sem, rc_sem,
):
    C, N, B, S, KV, G, HD, PG, PAGE, D = dims
    SS = S // N
    KC = max(1, KV // C)
    NB = KV // KC
    R = C // NB
    HS = KV * G // C
    U = SS * B * KC
    rows = U * G
    tokens = PG * PAGE
    scale = HD ** (-0.5) * math.log2(math.e)
    c = lax.axis_index("ctx")
    p = lax.axis_index("peer")
    own = c // R
    place = lax.rem(c, R)

    def block_of(i):
        return lax.rem(own + 1 + i, NB)

    loads = []
    for i in range(NB):
        heads = pl.ds(block_of(i) * KC, KC)
        loads.append((
            pltpu.make_async_copy(key_ref.at[:, :, heads], kbuf.at[i], k_sem.at[i]),
            pltpu.make_async_copy(value_ref.at[:, :, heads], vbuf.at[i], v_sem.at[i]),
        ))
    for pair in loads:
        pair[0].start()
        pair[1].start()
    width = D // C
    sub = width // N
    fine = sub % LANES == 0
    w_loads = []
    for k in range(C if fine else 1):
        start, size = (k * width + p * sub, sub) if fine else (p * (D // N), D // N)
        w_loads.append(pltpu.make_async_copy(
            weight_ref.at[:, pl.ds(pl.multiple_of(start, LANES), size)],
            wbuf.at[:, k * size:(k + 1) * size], w_sem.at[k],
        ))
    for load in w_loads:
        load.start()

    barrier = pltpu.get_barrier_semaphore()
    for dc in range(C):
        for dp in range(N):
            if dc or dp:
                pl.semaphore_signal(
                    barrier, inc=1,
                    device_id={"ctx": lax.rem(c + dc, C), "peer": lax.rem(p + dp, N)},
                    device_id_type=pl.DeviceIdType.MESH,
                )

    for b in range(B):
        for s in range(S):
            some = q_ref[b, s].astype(jnp.float32)
            for h in range(KV):
                qs[h, b, s * G:(s + 1) * G, :] = some[h * G:(h + 1) * G]
    first = (c * N + p) * PG
    ids = list_ref[...].reshape(B * S * KV, list_ref.shape[3])
    per_tile = LANES // PAGE
    lane_page = lax.broadcasted_iota(jnp.int32, (ids.shape[1], LANES), 1) // PAGE
    for j in range(tokens // LANES):
        listed = jnp.zeros((B * S * KV, LANES), jnp.float32)
        for k in range(per_tile):
            equal = jnp.where(ids == first + (j * per_tile + k), 1.0, 0.0).astype(jnp.bfloat16)
            spread = jnp.where(lane_page == k, 1.0, 0.0).astype(jnp.bfloat16)
            listed += jnp.dot(equal, spread, preferred_element_type=jnp.float32)
        mask[:, j * LANES:(j + 1) * LANES] = listed

    lane = lax.broadcasted_iota(jnp.int32, (G, LANES), 1)

    def attend(i):
        blk = block_of(i)
        tiles = [jnp.zeros((G, LANES), jnp.float32)] * N
        loads[i][0].wait()
        loads[i][1].wait()
        for b in range(B):
            for kc in range(KC):
                h = blk * KC + kc
                q = qs[h, b].astype(jnp.bfloat16)
                keys = kbuf[i, b, :, kc].reshape(tokens, HD)
                values = vbuf[i, b, :, kc].reshape(tokens, HD)
                score = lax.dot_general(
                    q, keys, (((1,), (1,)), ((), ())), preferred_element_type=jnp.float32
                )
                listed = jnp.concatenate([
                    jnp.broadcast_to(mask[pl.ds((b * S + s) * KV + h, 1), :], (G, tokens))
                    for s in range(S)
                ], axis=0)
                score = jnp.where(listed > 0.5, score * scale, masked_score)
                top = jnp.maximum(jnp.max(score, axis=1, keepdims=True), least_maximum)
                weights = jnp.exp2(score - top)
                total = jnp.sum(weights, axis=1, keepdims=True)
                blended = jnp.dot(
                    weights.astype(jnp.bfloat16), values, preferred_element_type=jnp.float32
                )
                for s in range(S):
                    n, ss = divmod(s, SS)
                    u = (ss * B + b) * KC + kc
                    part = slice(s * G, (s + 1) * G)
                    send_a[i, n, u * G:(u + 1) * G, :] = blended[part]
                    tiles[n] = jnp.where(
                        lane == u, top[part], jnp.where(lane == HALF + u, total[part], tiles[n])
                    )
        for n in range(N):
            send_a[i, n, rows:rows + G, :] = tiles[n]

    def copies_a(i):
        made = []
        for d in range(1, N):
            to = lax.rem(p + d, N)
            made.append(pltpu.make_async_remote_copy(
                src_ref=send_a.at[i, to], dst_ref=recv_a.at[i, d - 1],
                send_sem=sa_sem.at[i, d - 1], recv_sem=ra_sem.at[i, d - 1],
                device_id={"peer": to}, device_id_type=pl.DeviceIdType.MESH,
            ))
        return made

    def copies_b(i):
        made = []
        for dr in range(R):
            if i == NB - 1 and dr == 0:
                continue
            slot = i * R + dr - (1 if i == NB - 1 else 0)
            to = block_of(i) * R + lax.rem(place + dr, R)
            made.append(pltpu.make_async_remote_copy(
                src_ref=send_b.at[i], dst_ref=recv_b.at[slot],
                send_sem=sb_sem.at[slot], recv_sem=rb_sem.at[slot],
                device_id={"ctx": to}, device_id_type=pl.DeviceIdType.MESH,
            ))
        return made

    def factors(tiles):
        top = functools.reduce(jnp.maximum, tiles)
        scales = [jnp.exp2(t - top) for t in tiles]
        total = sum(f * pltpu.roll(t, HALF, 1) for f, t in zip(scales, tiles))
        return top, scales, total

    def blend(parts, scales, u):
        return sum(
            part[u * G:(u + 1) * G, :] * f[:, u:u + 1] for part, f in zip(parts, scales)
        )

    def fold_a(i):
        parts = [send_a.at[i, p]] + [recv_a.at[i, d] for d in range(N - 1)]
        tiles = [part[rows:rows + G, :] for part in parts]
        top, scales, total = factors(tiles)
        for u in range(U):
            send_b[i, u * G:(u + 1) * G, :] = blend(parts, scales, u)
        send_b[i, rows:rows + G, :] = jnp.where(lane < HALF, top, pltpu.roll(total, HALF, 1))

    all_a, all_b = [], []
    for i in range(NB + 1):
        if i < NB:
            attend(i)
            if i == 0:
                pl.semaphore_wait(barrier, C * N - 1)
            all_a.append(copies_a(i))
            for copy in all_a[i]:
                copy.start()
        if i > 0:
            for copy in all_a[i - 1]:
                copy.wait_recv()
            fold_a(i - 1)
            made = copies_b(i - 1)
            for copy in made:
                copy.start()
            all_b += made

    for copy in all_b:
        copy.wait_recv()
    parts = [send_b.at[NB - 1]] + [recv_b.at[d] for d in range(C - 1)]
    top, scales, total = factors([part[rows:rows + G, :] for part in parts])
    scales = [f / total for f in scales]
    mine = pl.ds(pl.multiple_of(p * rows, 8), rows)
    attended = jnp.concatenate([blend(parts, scales, u) for u in range(U)], axis=0)
    gat[mine, :] = attended
    all_g = []
    for d in range(1, N):
        to = lax.rem(p + d, N)
        all_g.append(pltpu.make_async_remote_copy(
            src_ref=gat.at[mine], dst_ref=gat.at[mine],
            send_sem=sg_sem.at[d - 1], recv_sem=rg_sem.at[d - 1],
            device_id={"peer": to}, device_id_type=pl.DeviceIdType.MESH,
        ))
    for copy in all_g:
        copy.start()
    for load in w_loads:
        load.wait()
    for d in range(1, N):
        theirs = gat.at[pl.ds(pl.multiple_of(lax.rem(p + N - d, N) * rows, 8), rows)]
        pltpu.make_async_remote_copy(
            src_ref=theirs, dst_ref=theirs,
            send_sem=sg_sem.at[d - 1], recv_sem=rg_sem.at[d - 1],
            device_id={"peer": lax.rem(p + d, N)}, device_id_type=pl.DeviceIdType.MESH,
        ).wait_recv()

    left = jnp.concatenate([
        gat[pl.ds((place * HS if R > 1 else 0) + j, S * B, stride=KC * G), :] for j in range(HS)
    ], axis=1).astype(jnp.bfloat16)
    product = jnp.dot(left, wbuf[...], preferred_element_type=jnp.float32)
    if fine:
        spread_fine(C, N, SS * B, sub, product, out_ref, send_c, recv_c, sc_sem, rc_sem)
    else:
        spread_coarse(C, N, SS * B, width, product, out_ref, send_c, recv_c, sc_sem, rc_sem)

    for copies in all_a:
        for copy in copies:
            copy.wait_send()
    for copy in all_b + all_g:
        copy.wait_send()


def spread_fine(C, N, count, sub, product, out_ref, send_c, recv_c, sc_sem, rc_sem):
    c = lax.axis_index("ctx")
    p = lax.axis_index("peer")
    for k in range(C):
        for n in range(N):
            send_c[k, n] = product[n * count:(n + 1) * count, k * sub:(k + 1) * sub]
    others = [(dc, dn) for dc in range(C) for dn in range(N) if dc or dn]
    copies = []
    for dc, dn in others:
        to_c, to_p = lax.rem(c + dc, C), lax.rem(p + dn, N)
        copies.append(pltpu.make_async_remote_copy(
            src_ref=send_c.at[to_c, to_p], dst_ref=recv_c.at[c, p],
            send_sem=sc_sem.at[dc, dn], recv_sem=rc_sem.at[dc, dn],
            device_id={"ctx": to_c, "peer": to_p}, device_id_type=pl.DeviceIdType.MESH,
        ))
    for copy in copies:
        copy.start()
    recv_c[c, p] = send_c[c, p]
    for (dc, dn) in others:
        from_c, from_p = lax.rem(c + C - dc, C), lax.rem(p + N - dn, N)
        pltpu.make_async_remote_copy(
            src_ref=send_c.at[from_c, from_p], dst_ref=recv_c.at[from_c, from_p],
            send_sem=sc_sem.at[dc, dn], recv_sem=rc_sem.at[dc, dn],
            device_id={"ctx": from_c, "peer": from_p}, device_id_type=pl.DeviceIdType.MESH,
        ).wait_recv()
    for n in range(N):
        out_ref[:, n * sub:(n + 1) * sub] = functools.reduce(
            jnp.add, [recv_c[k, n] for k in range(C)]
        )
    for copy in copies:
        copy.wait_send()


def spread_coarse(C, N, count, width, product, out_ref, send_c, recv_c, sc_sem, rc_sem):
    c = lax.axis_index("ctx")
    p = lax.axis_index("peer")
    Q = C // N
    for q in range(Q):
        for n in range(N):
            send_c[q, n] = product[n * count:(n + 1) * count, q * width:(q + 1) * width]

    def copy_c(q, dn):
        to = lax.rem(p + dn, N)
        return pltpu.make_async_remote_copy(
            src_ref=send_c.at[q, to], dst_ref=recv_c.at[c],
            send_sem=sc_sem.at[q, dn], recv_sem=rc_sem.at[c],
            device_id={"ctx": p * Q + q, "peer": to}, device_id_type=pl.DeviceIdType.MESH,
        )

    for q in range(Q):
        for dn in range(1, N):
            copy_c(q, dn).start()

        @pl.when(p * Q + q != c)
        def _():
            copy_c(q, 0).start()

        @pl.when(p * Q + q == c)
        def _():
            recv_c[c] = send_c[q, p]

    def wait_c(source):
        pltpu.make_async_remote_copy(
            src_ref=send_c.at[0, 0], dst_ref=recv_c.at[source],
            send_sem=sc_sem.at[0, 0], recv_sem=rc_sem.at[source],
            device_id={"ctx": source, "peer": c // Q}, device_id_type=pl.DeviceIdType.MESH,
        ).wait_recv()

    for dc in range(1, C):
        wait_c(lax.rem(c + dc, C))

    @pl.when(p != c // Q)
    def _():
        wait_c(c)

    out_ref[...] = functools.reduce(jnp.add, [recv_c[k] for k in range(C)])

    for q in range(Q):
        for dn in range(1, N):
            copy_c(q, dn).wait_send()

        @pl.when(p * Q + q != c)
        def _():
            copy_c(q, 0).wait_send()


def body(queries, key_cache, value_cache, page_list, out_weight):
    B, S, HQ, HD = queries.shape
    PG, KV, PAGE = key_cache.shape[1:4]
    D = out_weight.shape[1]
    C = lax.axis_size("ctx")
    N = lax.axis_size("peer")
    G = HQ // KV
    SS = S // N
    KC = max(1, KV // C)
    NB = KV // KC
    Q = C // N
    sub = D // C // N
    fine = sub % LANES == 0
    rows = SS * B * KC * G
    f32, bf16 = jnp.float32, jnp.bfloat16
    dma = pltpu.SemaphoreType.DMA
    dims = (C, N, B, S, KV, G, HD, PG, PAGE, D)
    vmem = pl.BlockSpec(memory_space=pltpu.VMEM)
    hbm = pl.BlockSpec(memory_space=pl.ANY)
    out = pl.pallas_call(
        functools.partial(kernel, dims),
        out_shape=jax.ShapeDtypeStruct((SS * B, D // C), f32),
        in_specs=[vmem, vmem, hbm, hbm, hbm],
        out_specs=vmem,
        scratch_shapes=[
            pltpu.VMEM((NB, B, PG, KC, PAGE, HD), bf16),
            pltpu.VMEM((NB, B, PG, KC, PAGE, HD), bf16),
            pltpu.VMEM((out_weight.shape[0], D // N), bf16),
            pltpu.VMEM((KV, B, S * G, HD), f32),
            pltpu.VMEM((B * S * KV, PG * PAGE), f32),
            pltpu.VMEM((NB, N, rows + G, HD), f32),
            pltpu.VMEM((NB, N - 1, rows + G, HD), f32),
            pltpu.VMEM((NB, rows + G, HD), f32),
            pltpu.VMEM((C - 1, rows + G, HD), f32),
            pltpu.VMEM((N * rows, HD), f32),
            pltpu.VMEM((C, N, SS * B, sub) if fine else (Q, N, SS * B, D // C), f32),
            pltpu.VMEM((C, N, SS * B, sub) if fine else (C, SS * B, D // C), f32),
            dma((NB,)), dma((NB,)), dma((C,)),
            dma((NB, N - 1)), dma((NB, N - 1)),
            dma((C - 1,)), dma((C - 1,)),
            dma((N - 1,)), dma((N - 1,)),
            dma((C, N) if fine else (Q, N)), dma((C, N) if fine else (C,)),
        ],
        compiler_params=pltpu.CompilerParams(
            collective_id=0, has_side_effects=True, vmem_limit_bytes=63 * 2**20
        ),
        name="paged_attention_projection",
    )(queries, page_list, key_cache, value_cache, out_weight)
    return out.reshape(SS, B, D // C).swapaxes(0, 1)


def solution(mesh):
    in_specs = (
        P("groups", None, None, None),
        P("groups", ("ctx", "peer"), None, None, None),
        P("groups", ("ctx", "peer"), None, None, None),
        P("groups", None, None, None),
        P("ctx", None),
    )
    out_specs = P("groups", "peer", "ctx")
    return jax.shard_map(body, mesh=mesh, in_specs=in_specs, out_specs=out_specs, check_vma=False)
```

```python
import functools
import math

import jax
import jax.numpy as jnp
from jax import lax
from jax.experimental import pallas as pl
from jax.experimental.pallas import tpu as pltpu
from jax.sharding import PartitionSpec as P

masked_score = -1e30
least_maximum = -1e20
LANES = 128
HALF = LANES // 2


def kernel(
    dims,
    q_ref, list_ref, key_ref, value_ref, weight_ref, out_ref,
    kbuf, vbuf, wbuf, qs, mask, send_a, recv_a, send_b, recv_b, gat, send_c, recv_c,
    k_sem, v_sem, w_sem, sa_sem, ra_sem, sb_sem, rb_sem, sg_sem, rg_sem, sc_sem, rc_sem,
):
    C, N, B, S, KV, G, HD, PG, PAGE, D = dims
    SS = S // N
    KC = max(1, KV // C)
    NB = KV // KC
    R = C // NB
    HS = KV * G // C
    U = SS * B * KC
    rows = U * G
    tokens = PG * PAGE
    scale = HD ** (-0.5) * math.log2(math.e)
    c = lax.axis_index("ctx")
    p = lax.axis_index("peer")
    own = c // R
    place = lax.rem(c, R)

    def block_of(i):
        return lax.rem(own + 1 + i, NB)

    loads = []
    for i in range(NB):
        heads = pl.ds(block_of(i) * KC, KC)
        loads.append((
            pltpu.make_async_copy(key_ref.at[:, :, heads], kbuf.at[i], k_sem.at[i]),
            pltpu.make_async_copy(value_ref.at[:, :, heads], vbuf.at[i], v_sem.at[i]),
        ))
    for pair in loads:
        pair[0].start()
        pair[1].start()
    width = D // C
    sub = width // N
    fine = sub % LANES == 0
    w_loads = []
    for k in range(C if fine else 1):
        start, size = (k * width + p * sub, sub) if fine else (p * (D // N), D // N)
        w_loads.append(pltpu.make_async_copy(
            weight_ref.at[:, pl.ds(pl.multiple_of(start, LANES), size)],
            wbuf.at[:, k * size:(k + 1) * size], w_sem.at[k],
        ))
    for load in w_loads:
        load.start()

    barrier = pltpu.get_barrier_semaphore()
    for dc in range(C):
        for dp in range(N):
            if dc or dp:
                pl.semaphore_signal(
                    barrier, inc=1,
                    device_id={"ctx": lax.rem(c + dc, C), "peer": lax.rem(p + dp, N)},
                    device_id_type=pl.DeviceIdType.MESH,
                )

    for b in range(B):
        for s in range(S):
            some = q_ref[b, s].astype(jnp.float32)
            for h in range(KV):
                qs[h, b, s * G:(s + 1) * G, :] = some[h * G:(h + 1) * G]
    first = (c * N + p) * PG
    ids = list_ref[...].reshape(B * S * KV, list_ref.shape[3])
    per_tile = LANES // PAGE
    lane_page = lax.broadcasted_iota(jnp.int32, (ids.shape[1], LANES), 1) // PAGE
    for j in range(tokens // LANES):
        listed = jnp.zeros((B * S * KV, LANES), jnp.float32)
        for k in range(per_tile):
            equal = jnp.where(ids == first + (j * per_tile + k), 1.0, 0.0).astype(jnp.bfloat16)
            spread = jnp.where(lane_page == k, 1.0, 0.0).astype(jnp.bfloat16)
            listed += jnp.dot(equal, spread, preferred_element_type=jnp.float32)
        mask[:, j * LANES:(j + 1) * LANES] = listed

    lane = lax.broadcasted_iota(jnp.int32, (G, LANES), 1)

    def attend(i):
        blk = block_of(i)
        tiles = [jnp.zeros((G, LANES), jnp.float32)] * N
        loads[i][0].wait()
        loads[i][1].wait()
        for b in range(B):
            for kc in range(KC):
                h = blk * KC + kc
                q = qs[h, b].astype(jnp.bfloat16)
                keys = kbuf[i, b, :, kc].reshape(tokens, HD)
                values = vbuf[i, b, :, kc].reshape(tokens, HD)
                score = lax.dot_general(
                    q, keys, (((1,), (1,)), ((), ())), preferred_element_type=jnp.float32
                )
                listed = jnp.concatenate([
                    jnp.broadcast_to(mask[pl.ds((b * S + s) * KV + h, 1), :], (G, tokens))
                    for s in range(S)
                ], axis=0)
                score = jnp.where(listed > 0.5, score * scale, masked_score)
                top = jnp.maximum(jnp.max(score, axis=1, keepdims=True), least_maximum)
                weights = jnp.exp2(score - top)
                total = jnp.sum(weights, axis=1, keepdims=True)
                blended = jnp.dot(
                    weights.astype(jnp.bfloat16), values, preferred_element_type=jnp.float32
                )
                for s in range(S):
                    n, ss = divmod(s, SS)
                    u = (ss * B + b) * KC + kc
                    part = slice(s * G, (s + 1) * G)
                    send_a[i, n, u * G:(u + 1) * G, :] = blended[part]
                    tiles[n] = jnp.where(
                        lane == u, top[part], jnp.where(lane == HALF + u, total[part], tiles[n])
                    )
        for n in range(N):
            send_a[i, n, rows:rows + G, :] = tiles[n]

    def copies_a(i):
        made = []
        for d in range(1, N):
            to = lax.rem(p + d, N)
            made.append(pltpu.make_async_remote_copy(
                src_ref=send_a.at[i, to], dst_ref=recv_a.at[i, d - 1],
                send_sem=sa_sem.at[i, d - 1], recv_sem=ra_sem.at[i, d - 1],
                device_id={"peer": to}, device_id_type=pl.DeviceIdType.MESH,
            ))
        return made

    def copies_b(i):
        made = []
        for dr in range(R):
            if i == NB - 1 and dr == 0:
                continue
            slot = i * R + dr - (1 if i == NB - 1 else 0)
            to = block_of(i) * R + lax.rem(place + dr, R)
            made.append(pltpu.make_async_remote_copy(
                src_ref=send_b.at[i], dst_ref=recv_b.at[slot],
                send_sem=sb_sem.at[slot], recv_sem=rb_sem.at[slot],
                device_id={"ctx": to}, device_id_type=pl.DeviceIdType.MESH,
            ))
        return made

    def factors(tiles):
        top = functools.reduce(jnp.maximum, tiles)
        scales = [jnp.exp2(t - top) for t in tiles]
        total = sum(f * pltpu.roll(t, HALF, 1) for f, t in zip(scales, tiles))
        return top, scales, total

    def blend(parts, scales, u):
        return sum(
            part[u * G:(u + 1) * G, :] * f[:, u:u + 1] for part, f in zip(parts, scales)
        )

    def fold_a(i):
        parts = [send_a.at[i, p]] + [recv_a.at[i, d] for d in range(N - 1)]
        tiles = [part[rows:rows + G, :] for part in parts]
        top, scales, total = factors(tiles)
        for u in range(U):
            send_b[i, u * G:(u + 1) * G, :] = blend(parts, scales, u)
        send_b[i, rows:rows + G, :] = jnp.where(lane < HALF, top, pltpu.roll(total, HALF, 1))

    all_a, all_b = [], []
    for i in range(NB + 1):
        if i < NB:
            attend(i)
            if i == 0:
                pl.semaphore_wait(barrier, C * N - 1)
            all_a.append(copies_a(i))
            for copy in all_a[i]:
                copy.start()
        if i > 0:
            for copy in all_a[i - 1]:
                copy.wait_recv()
            fold_a(i - 1)
            made = copies_b(i - 1)
            for copy in made:
                copy.start()
            all_b += made

    for copy in all_b:
        copy.wait_recv()
    parts = [send_b.at[NB - 1]] + [recv_b.at[d] for d in range(C - 1)]
    top, scales, total = factors([part[rows:rows + G, :] for part in parts])
    scales = [f / total for f in scales]
    mine = pl.ds(pl.multiple_of(p * rows, 8), rows)
    attended = jnp.concatenate([blend(parts, scales, u) for u in range(U)], axis=0)
    gat[mine, :] = attended
    all_g = []
    for d in range(1, N):
        to = lax.rem(p + d, N)
        all_g.append(pltpu.make_async_remote_copy(
            src_ref=gat.at[mine], dst_ref=gat.at[mine],
            send_sem=sg_sem.at[d - 1], recv_sem=rg_sem.at[d - 1],
            device_id={"peer": to}, device_id_type=pl.DeviceIdType.MESH,
        ))
    for copy in all_g:
        copy.start()
    for load in w_loads:
        load.wait()
    for d in range(1, N):
        theirs = gat.at[pl.ds(pl.multiple_of(lax.rem(p + N - d, N) * rows, 8), rows)]
        pltpu.make_async_remote_copy(
            src_ref=theirs, dst_ref=theirs,
            send_sem=sg_sem.at[d - 1], recv_sem=rg_sem.at[d - 1],
            device_id={"peer": lax.rem(p + d, N)}, device_id_type=pl.DeviceIdType.MESH,
        ).wait_recv()

    left = jnp.concatenate([
        gat[pl.ds((place * HS if R > 1 else 0) + j, S * B, stride=KC * G), :] for j in range(HS)
    ], axis=1).astype(jnp.bfloat16)
    product = jnp.dot(left, wbuf[...], preferred_element_type=jnp.float32)
    if fine:
        spread_fine(C, N, SS * B, sub, product, out_ref, send_c, recv_c, sc_sem, rc_sem)
    else:
        spread_coarse(C, N, SS * B, width, product, out_ref, send_c, recv_c, sc_sem, rc_sem)

    for copies in all_a:
        for copy in copies:
            copy.wait_send()
    for copy in all_b + all_g:
        copy.wait_send()


def spread_fine(C, N, count, sub, product, out_ref, send_c, recv_c, sc_sem, rc_sem):
    c = lax.axis_index("ctx")
    p = lax.axis_index("peer")
    for k in range(C):
        for n in range(N):
            send_c[k, n] = product[n * count:(n + 1) * count, k * sub:(k + 1) * sub]
    others = [(dc, dn) for dc in range(C) for dn in range(N) if dc or dn]
    copies = []
    for dc, dn in others:
        to_c, to_p = lax.rem(c + dc, C), lax.rem(p + dn, N)
        copies.append(pltpu.make_async_remote_copy(
            src_ref=send_c.at[to_c, to_p], dst_ref=recv_c.at[c, p],
            send_sem=sc_sem.at[dc, dn], recv_sem=rc_sem.at[dc, dn],
            device_id={"ctx": to_c, "peer": to_p}, device_id_type=pl.DeviceIdType.MESH,
        ))
    for copy in copies:
        copy.start()
    recv_c[c, p] = send_c[c, p]
    for (dc, dn) in others:
        from_c, from_p = lax.rem(c + C - dc, C), lax.rem(p + N - dn, N)
        pltpu.make_async_remote_copy(
            src_ref=send_c.at[from_c, from_p], dst_ref=recv_c.at[from_c, from_p],
            send_sem=sc_sem.at[dc, dn], recv_sem=rc_sem.at[dc, dn],
            device_id={"ctx": from_c, "peer": from_p}, device_id_type=pl.DeviceIdType.MESH,
        ).wait_recv()
    for n in range(N):
        whole = functools.reduce(jnp.add, [recv_c[k, n] for k in range(C)])
        B = out_ref.shape[0]
        for r in range(count):
            out_ref[r % B, r // B:r // B + 1, n * sub:(n + 1) * sub] = whole[r:r + 1]
    for copy in copies:
        copy.wait_send()


def spread_coarse(C, N, count, width, product, out_ref, send_c, recv_c, sc_sem, rc_sem):
    c = lax.axis_index("ctx")
    p = lax.axis_index("peer")
    Q = C // N
    for q in range(Q):
        for n in range(N):
            send_c[q, n] = product[n * count:(n + 1) * count, q * width:(q + 1) * width]

    def copy_c(q, dn):
        to = lax.rem(p + dn, N)
        return pltpu.make_async_remote_copy(
            src_ref=send_c.at[q, to], dst_ref=recv_c.at[c],
            send_sem=sc_sem.at[q, dn], recv_sem=rc_sem.at[c],
            device_id={"ctx": p * Q + q, "peer": to}, device_id_type=pl.DeviceIdType.MESH,
        )

    for q in range(Q):
        for dn in range(1, N):
            copy_c(q, dn).start()

        @pl.when(p * Q + q != c)
        def _():
            copy_c(q, 0).start()

        @pl.when(p * Q + q == c)
        def _():
            recv_c[c] = send_c[q, p]

    def wait_c(source):
        pltpu.make_async_remote_copy(
            src_ref=send_c.at[0, 0], dst_ref=recv_c.at[source],
            send_sem=sc_sem.at[0, 0], recv_sem=rc_sem.at[source],
            device_id={"ctx": source, "peer": c // Q}, device_id_type=pl.DeviceIdType.MESH,
        ).wait_recv()

    for dc in range(1, C):
        wait_c(lax.rem(c + dc, C))

    @pl.when(p != c // Q)
    def _():
        wait_c(c)

    whole = functools.reduce(jnp.add, [recv_c[k] for k in range(C)])
    B = out_ref.shape[0]
    for r in range(count):
        out_ref[r % B, r // B:r // B + 1, :] = whole[r:r + 1]

    for q in range(Q):
        for dn in range(1, N):
            copy_c(q, dn).wait_send()

        @pl.when(p * Q + q != c)
        def _():
            copy_c(q, 0).wait_send()


def body(queries, key_cache, value_cache, page_list, out_weight):
    B, S, HQ, HD = queries.shape
    PG, KV, PAGE = key_cache.shape[1:4]
    D = out_weight.shape[1]
    C = lax.axis_size("ctx")
    N = lax.axis_size("peer")
    G = HQ // KV
    SS = S // N
    KC = max(1, KV // C)
    NB = KV // KC
    Q = C // N
    sub = D // C // N
    fine = sub % LANES == 0
    rows = SS * B * KC * G
    f32, bf16 = jnp.float32, jnp.bfloat16
    dma = pltpu.SemaphoreType.DMA
    dims = (C, N, B, S, KV, G, HD, PG, PAGE, D)
    vmem = pl.BlockSpec(memory_space=pltpu.VMEM)
    hbm = pl.BlockSpec(memory_space=pl.ANY)
    out = pl.pallas_call(
        functools.partial(kernel, dims),
        out_shape=jax.ShapeDtypeStruct((B, SS, D // C), f32),
        in_specs=[vmem, vmem, hbm, hbm, hbm],
        out_specs=vmem,
        scratch_shapes=[
            pltpu.VMEM((NB, B, PG, KC, PAGE, HD), bf16),
            pltpu.VMEM((NB, B, PG, KC, PAGE, HD), bf16),
            pltpu.VMEM((out_weight.shape[0], D // N), bf16),
            pltpu.VMEM((KV, B, S * G, HD), f32),
            pltpu.VMEM((B * S * KV, PG * PAGE), f32),
            pltpu.VMEM((NB, N, rows + G, HD), f32),
            pltpu.VMEM((NB, N - 1, rows + G, HD), f32),
            pltpu.VMEM((NB, rows + G, HD), f32),
            pltpu.VMEM((C - 1, rows + G, HD), f32),
            pltpu.VMEM((N * rows, HD), f32),
            pltpu.VMEM((C, N, SS * B, sub) if fine else (Q, N, SS * B, D // C), f32),
            pltpu.VMEM((C, N, SS * B, sub) if fine else (C, SS * B, D // C), f32),
            dma((NB,)), dma((NB,)), dma((C,)),
            dma((NB, N - 1)), dma((NB, N - 1)),
            dma((C - 1,)), dma((C - 1,)),
            dma((N - 1,)), dma((N - 1,)),
            dma((C, N) if fine else (Q, N)), dma((C, N) if fine else (C,)),
        ],
        compiler_params=pltpu.CompilerParams(
            collective_id=0, has_side_effects=True, vmem_limit_bytes=63 * 2**20
        ),
        name="paged_attention_projection",
    )(queries, page_list, key_cache, value_cache, out_weight)
    return out


def solution(mesh):
    in_specs = (
        P("groups", None, None, None),
        P("groups", ("ctx", "peer"), None, None, None),
        P("groups", ("ctx", "peer"), None, None, None),
        P("groups", None, None, None),
        P("ctx", None),
    )
    out_specs = P("groups", "peer", "ctx")
    return jax.shard_map(body, mesh=mesh, in_specs=in_specs, out_specs=out_specs, check_vma=False)
```
